32 devices in a mesh: grp: 2 (over y), cuts: 4 (over z), space: 4 (over x, core).
Axes of the slice: x: 2, y: 2, z: 4, core: 2. Of those that a mesh axis runs over, the one named last changes fastest.
Arguments:
- left_modes: float32 [8, 1024, 1024], P(('grp', 'cuts'), None, 'space'), parts along dimension 0, may hold values from -0.25 to 0.25
- right_modes: float32 [8, 1024, 1024], P(('grp', 'cuts'), None, 'space'), parts along dimension 0, may hold values from -6 to 6
- momenta: int32 [4, 3], replicated, may hold values from -2 to 2
- partners: int32 [4], replicated, may hold values from 0 to 3, as said below
Outputs:
- meson_field: float32 [8, 1024, 4, 1024], P(('grp', 'cuts'), 'space'), parts along dimension 0
- product: float32 [8, 1024, 4, 1024], P(('grp', 'cuts'), 'space'), parts along dimension 0
The draws below stay inside these ranges and needn't reach their ends.
There are 2 independent parts, one for each index of `grp`. The reference program is written for one: setup_inputs(seed, part) draws one part's arguments, and reference() takes and returns one part's arrays. A program takes and returns all parts, laid end to end along the dimension named above; an argument that names none is the same for every part. Nothing has to cross between parts.
Inputs may be any that keep to these rules, and one draw needn't show every extreme that they name: `partners`: every slice is named exactly once.
All inputs are finite; a program needn't handle non-finite values.
Results may differ from the reference program's by a relative error of at most 0.00011.
Values sent between devices are 32-bit elements; how exact they have to be, the bound alone decides.
A program may use at most 64 MiB of HBM per device.

```python
import math
import jax
import jax.numpy as jnp
from jax import lax

MODES = 1024
VERTS = 4
NT = 4
SITES = 1024


def force_entry(table, where, target):
    holder = jnp.argmax((table == target).astype(jnp.int32)).astype(jnp.int32)
    before = table[where]
    table = table.at[holder].set(before)
    return table.at[where].set(target)


def draw_partners(key, part):
    order_key = jax.random.fold_in(key, 11)
    pick_key = jax.random.fold_in(key, 12)
    table = jax.random.permutation(order_key, NT).astype(jnp.int32)
    chosen = jax.random.randint(pick_key, (), 0, NT).astype(jnp.int32)
    table = force_entry(table, chosen, (chosen + NT - 1) % NT)
    second = (chosen + 1) % NT
    table = force_entry(table, second, (second + NT // 2) % NT)
    return table.astype(jnp.int32)


def touch_ends(result, own_key, smallest, top_value):
    longest = result.shape.index(max(result.shape))
    spots = []
    for shift in (0, 1):
        where = [jax.random.randint(jax.random.fold_in(own_key, axis), (), 0, length) for axis, length in enumerate(result.shape)]
        where[longest] = (where[longest] + shift) % result.shape[longest]
        spots.append(tuple(where))
    return result.at[spots[0]].set(smallest).at[spots[1]].set(top_value)


def raised(result, stream_key, source, target, parts, factor):
    owner, partner = [(jnp.arange(result.shape[axis_at]) // (result.shape[axis_at] // parts)).reshape([-1 if axis == axis_at else 1 for axis in range(result.ndim)]) for axis_at in (source, target)]
    chosen = jax.random.permutation(stream_key, parts)[partner]
    strong = (owner == chosen) | (owner == (partner + parts // 2) % parts)
    return jnp.where(strong, factor * result, result)


def steps_of(own_key, extent, pieces, smallest, top_value):
    loudness, own = 1.0, jax.random.fold_in(own_key, 6)
    for position, shards_of in pieces:
        heights = jnp.exp(jax.random.uniform(jax.random.fold_in(own, position), (shards_of,), jnp.float32, smallest / len(pieces), top_value / len(pieces)))
        loudness = loudness * jnp.repeat(heights, extent[position] // shards_of).reshape([-1 if axis == position else 1 for axis in range(len(extent))])
    return loudness


def normal_values(rng, extent, spread, bound, pieces=(), held_as=jnp.bfloat16):
    factor_of = steps_of(rng, extent, pieces, -0.22, 0.18) if pieces else 1.0
    drawn = jax.random.normal(rng, extent, jnp.float32) * spread * factor_of
    return jnp.minimum(jnp.maximum(drawn, -bound), bound).astype(held_as)


def noise_with(key, shape, scale, limit, cuts, heavy, kind=jnp.bfloat16):
    drawn = scale * jax.random.normal(key, shape, jnp.float32)
    if cuts:
        drawn = drawn * steps_of(key, shape, cuts, -0.22, 0.18)
    return jnp.clip(raised(drawn, jax.random.fold_in(key, 3), *heavy), -limit, limit).astype(kind)


def setup_inputs(seed: int = 0, part: int = 0) -> dict:
    seeds = jax.random.split(jax.random.key(seed), 5)
    part_splits = jax.random.split(jax.random.fold_in(seeds[4], part), 5)
    return {
        "left_modes": noise_with(part_splits[0], (NT, MODES, SITES), SITES ** -0.5, 0.25, ((0, 4), (2, 4)), (2, 1, 4, 2.0), jnp.float32),
        "right_modes": normal_values(part_splits[1], (NT, MODES, SITES), 1.0, 6.0, ((0, 4), (2, 4)), jnp.float32),
        "momenta": touch_ends(jax.random.randint(seeds[2], (VERTS, 3), -2, 3), jax.random.fold_in(seeds[2], 1), -2, 2).astype(jnp.int32),
        "partners": draw_partners(jax.random.fold_in(seeds[4], 71), part),
    }


def phase_table(momenta, offset, amount, site_total):
    global_site = offset + jnp.arange(amount, dtype=jnp.int32)
    coord_x = global_site % 8
    coord_y = global_site // 8 % 8
    coord_z = global_site // 64
    depth = site_total // 64
    numerator = ((momenta[:, 0:1] * coord_x[None] + momenta[:, 1:2] * coord_y[None]) * depth + momenta[:, 2:3] * coord_z[None] * 8) % (8 * depth)
    return jnp.cos(2.0 * math.pi * numerator.astype(jnp.float32) / (8 * depth))

def reference(left_modes, right_modes, momenta, partners):
    phases = phase_table(momenta, jnp.int32(0), SITES, SITES)

    def one_slice(index):
        weighted = left_modes[index][:, None, :] * phases[None]
        return jnp.einsum('max,nx->man', weighted, right_modes[index], precision=lax.Precision.HIGHEST)
    meson_field = lax.map(one_slice, jnp.arange(NT, dtype=jnp.int32))
    first_vertex = meson_field[partners][:, :, 0, :]
    product = jnp.einsum('tmak,tkn->tman', meson_field, first_vertex, precision=lax.Precision.HIGHEST) * (1.0 / math.sqrt(MODES))
    return (meson_field, product)
```

```python
import functools
import math

import jax
import jax.numpy as jnp
from jax import lax
from jax.experimental import pallas as pl
from jax.experimental.pallas import tpu as pltpu
from jax.sharding import PartitionSpec as P

MODES = 1024
CHUNKS = 4


def phase_table(momenta, site_total):
    global_site = jnp.arange(site_total, dtype=jnp.int32)
    coord_x = global_site % 8
    coord_y = global_site // 8 % 8
    coord_z = global_site // 64
    depth = site_total // 64
    numerator = (
        (momenta[:, 0:1] * coord_x[None] + momenta[:, 1:2] * coord_y[None]) * depth
        + momenta[:, 2:3] * coord_z[None] * 8
    ) % (8 * depth)
    return jnp.cos(2.0 * math.pi * numerator.astype(jnp.float32) / (8 * depth))


def split(value):
    high = value.astype(jnp.bfloat16)
    return high, (value - high.astype(jnp.float32)).astype(jnp.bfloat16)


def dot3(a_high, a_low, b_high, b_low, b_axis):
    dims = (((1,), (b_axis,)), ((), ()))
    dot = functools.partial(
        lax.dot_general, dimension_numbers=dims, preferred_element_type=jnp.float32
    )
    return dot(a_low, b_high) + dot(a_high, b_low) + dot(a_high, b_high)


def kernel(
    slices, space_size, scale,
    partners_ref, phase_ref, left_ref, right_ref,
    meson_ref, product_ref,
    left_far, left_peer, right_far, right_peer,
    w_high, w_low, r_high, r_low, m_high, m_low,
    route, field_far, field_peer, f_high, f_low,
    lf_sem, lp_sem, rf_sem, rp_sem, z_sem, ff_sem, fp_sem,
):
    mode_total, site_local = left_ref.shape
    verts = phase_ref.shape[0]
    rows = mode_total // space_size
    chips = space_size // 2
    width = mode_total // CHUNKS
    far = range(1, chips)

    me = lax.axis_index("space")
    zed = lax.axis_index("cuts")
    chip, core = me // 2, me % 2
    peer = chip * 2 + 1 - core

    def far_device(d):
        return lax.rem(chip + d, chips) * 2 + core

    def source(d, k):
        from_chip = lax.rem(chip + chips - d, chips)
        return from_chip * 2 + (core if k == 0 else 1 - core)

    def remote(src, dst, sems, where, axis, target):
        return pltpu.make_async_remote_copy(
            src_ref=src,
            dst_ref=dst,
            send_sem=sems.at[(0,) + where],
            recv_sem=sems.at[(1,) + where],
            device_id={axis: target},
            device_id_type=pl.DeviceIdType.MESH,
        )

    barrier = pltpu.get_barrier_semaphore()

    def greet(axis, target):
        pl.semaphore_signal(
            barrier, inc=1, device_id={axis: target}, device_id_type=pl.DeviceIdType.MESH
        )

    greet("space", peer)
    for d in far:
        greet("space", far_device(d))

    @pl.when(zed > 0)
    def _():
        greet("cuts", zed - 1)

    @pl.when(zed < slices - 1)
    def _():
        greet("cuts", zed + 1)

    ends = jnp.where(zed > 0, 1, 0) + jnp.where(zed < slices - 1, 1, 0)
    pl.semaphore_wait(barrier, chips + ends)

    def rows_of(ref, index, count):
        return ref.at[pl.ds(pl.multiple_of(index * count, count), count), :]

    def chunk_of(ref, j):
        return ref.at[pl.ds(j * width, width), :]

    left_far_copy = {
        d: remote(
            rows_of(left_ref, lax.rem(chip + d, chips), 2 * rows),
            left_far.at[d - 1], lf_sem, (d - 1,), "space", far_device(d),
        )
        for d in far
    }
    right_far_copy = {
        (d, j): remote(
            chunk_of(right_ref, j), chunk_of(right_far.at[d - 1], j),
            rf_sem, (d - 1, j), "space", far_device(d),
        )
        for d in far for j in range(CHUNKS)
    }
    left_peer_copy = {
        d: remote(
            rows_of(left_ref, peer, rows) if d == 0 else rows_of(left_far.at[d - 1], 1 - core, rows),
            left_peer.at[d], lp_sem, (d,), "space", peer,
        )
        for d in range(chips)
    }
    right_peer_copy = {
        (d, j): remote(
            chunk_of(right_ref if d == 0 else right_far.at[d - 1], j),
            chunk_of(right_peer.at[d], j), rp_sem, (d, j), "space", peer,
        )
        for d in range(chips) for j in range(CHUNKS)
    }

    def z_copy(j, r):
        up = zed % 2 == r % 2
        other = jnp.where(up, zed + 1, zed - 1)
        has = (other >= 0) & (other < slices)
        return has, remote(route.at[j, r, 0], route.at[j, r, 1], z_sem, (j, r), "cuts", other)

    field_far_copy = {
        (d, j): remote(
            route.at[j, slices, 0], field_far.at[j, d - 1], ff_sem, (d - 1, j), "space", far_device(d)
        )
        for d in far for j in range(CHUNKS)
    }
    field_peer_copy = {
        (d, j): remote(
            route.at[j, slices, 0] if d == 0 else field_far.at[j, d - 1],
            field_peer.at[j, d], fp_sem, (d, j), "space", peer,
        )
        for d in range(chips) for j in range(CHUNKS)
    }

    for d in far:
        left_far_copy[d].start()
    left_peer_copy[0].start()
    for j in range(CHUNKS):
        for d in far:
            right_far_copy[d, j].start()
        right_peer_copy[0, j].start()

    keys = []
    for u in range(slices):
        key = jnp.int32(0)
        for t in range(slices):
            key = key + jnp.where(partners_ref[t] == u, t, 0)
        keys.append(key)
    takes = []
    for r in range(slices):
        take = jnp.int32(0)
        for i in range(r % 2, slices - 1, 2):
            low, high = jnp.minimum(keys[i], keys[i + 1]), jnp.maximum(keys[i], keys[i + 1])
            swap = jnp.where(keys[i] > keys[i + 1], 1, 0)
            mine = jnp.where((zed == i) | (zed == i + 1), 1, 0)
            take = take + swap * mine
            keys[i], keys[i + 1] = low, high
        takes.append(take)

    def weigh(d, k, block):
        at = (2 * d + k) * site_local
        first = pl.multiple_of(source(d, k) * site_local, site_local)
        for a in range(verts):
            high, low = split(block * phase_ref[pl.ds(a, 1), pl.ds(first, site_local)])
            w_high[a, :, pl.ds(at, site_local)] = high
            w_low[a, :, pl.ds(at, site_local)] = low

    def own_rows(ref, index):
        return ref[pl.ds(pl.multiple_of(index * rows, rows), rows), :]

    weigh(0, 0, own_rows(left_ref, me))
    left_peer_copy[0].wait_recv()
    weigh(0, 1, left_peer[0])
    for d in far:
        left_far_copy[d].wait_recv()
        left_peer_copy[d].start()
        weigh(d, 0, own_rows(left_far.at[d - 1], core))
    for d in far:
        left_peer_copy[d].wait_recv()
        weigh(d, 1, left_peer[d])

    def split_right(d, k, block):
        at = (2 * d + k) * site_local
        high, low = split(block)
        r_high[:, pl.ds(at, site_local)] = high
        r_low[:, pl.ds(at, site_local)] = low

    def meson_block(a, j):
        block = dot3(w_high[a], w_low[a], r_high[...], r_low[...], 1)
        columns = pl.ds(j * width, width)
        meson_ref[a, :, columns] = block
        high, low = split(block)
        m_high[a, :, columns] = high
        m_low[a, :, columns] = low
        return block

    def z_start(j, r):
        has, copy = z_copy(j, r)

        @pl.when(has)
        def _():
            copy.start()

    def fields(j):
        split_right(0, 0, right_ref[pl.ds(j * width, width), :])
        right_peer_copy[0, j].wait_recv()
        split_right(0, 1, right_peer[0, pl.ds(j * width, width), :])
        for d in far:
            right_far_copy[d, j].wait_recv()
            right_peer_copy[d, j].start()
            split_right(d, 0, right_far[d - 1, pl.ds(j * width, width), :])
        for d in far:
            right_peer_copy[d, j].wait_recv()
            split_right(d, 1, right_peer[d, pl.ds(j * width, width), :])
        route[j, 0, 0] = meson_block(0, j)
        z_start(j, 0)

        def other_vertex(a, carry):
            meson_block(a, j)
            return carry

        lax.fori_loop(1, verts, other_vertex, 0)

    def z_round(j, r):
        has, copy = z_copy(j, r)

        @pl.when(has)
        def _():
            copy.wait_recv()
            taken = jnp.full((rows, width), takes[r], jnp.int32) > 0
            route[j, r + 1, 0] = jnp.where(taken, route[j, r, 1], route[j, r, 0])

        @pl.when(jnp.logical_not(has))
        def _():
            route[j, r + 1, 0] = route[j, r, 0]

        if r + 1 < slices:
            z_start(j, r + 1)
        else:
            for d in far:
                field_far_copy[d, j].start()
            field_peer_copy[0, j].start()

    def pass_on(j):
        for d in far:
            field_far_copy[d, j].wait_recv()
            field_peer_copy[d, j].start()

    def products(j):
        def place(d, k, block):
            first = pl.multiple_of(source(d, k) * rows, rows)
            high, low = split(block)
            f_high[pl.ds(first, rows), :] = high
            f_low[pl.ds(first, rows), :] = low

        place(0, 0, route[j, slices, 0])
        for d in far:
            place(d, 0, field_far[j, d - 1])
        for d in range(chips):
            field_peer_copy[d, j].wait_recv()
            place(d, 1, field_peer[j, d])

        def vertex(a, carry):
            block = dot3(m_high[a], m_low[a], f_high[...], f_low[...], 0)
            product_ref[a, :, pl.ds(j * width, width)] = block * scale
            return carry

        lax.fori_loop(0, verts, vertex, 0)

    for step in range(CHUNKS + slices + 2):
        if step < CHUNKS:
            fields(step)
        for r in reversed(range(slices)):
            if 0 <= step - 1 - r < CHUNKS:
                z_round(step - 1 - r, r)
        if 0 <= step - 1 - slices < CHUNKS:
            pass_on(step - 1 - slices)
        if 0 <= step - 2 - slices < CHUNKS:
            products(step - 2 - slices)

    for copies in (
        left_far_copy, right_far_copy, left_peer_copy, right_peer_copy,
        field_far_copy, field_peer_copy,
    ):
        for copy in copies.values():
            copy.wait_send()
    for j in range(CHUNKS):
        for r in range(slices):
            has, copy = z_copy(j, r)

            @pl.when(has)
            def _(copy=copy):
                copy.wait_send()


def on_device(left_modes, right_modes, momenta, partners):
    left_local, right_local = left_modes[0], right_modes[0]
    mode_total, site_local = left_local.shape
    space_size = lax.axis_size("space")
    slices = lax.axis_size("cuts")
    verts = momenta.shape[0]
    rows = mode_total // space_size
    chips = space_size // 2
    others = max(chips - 1, 1)
    width = mode_total // CHUNKS
    depth = site_local * space_size
    phases = phase_table(momenta, depth)
    f32, bf16 = jnp.float32, jnp.bfloat16
    vmem = pl.BlockSpec(memory_space=pltpu.VMEM)
    out = jax.ShapeDtypeStruct((verts, rows, mode_total), f32)

    def dma(*shape):
        return pltpu.SemaphoreType.DMA((2,) + shape)

    meson, product = pl.pallas_call(
        functools.partial(kernel, slices, space_size, 1.0 / math.sqrt(mode_total)),
        out_shape=(out, out),
        in_specs=[pl.BlockSpec(memory_space=pltpu.SMEM), vmem, vmem, vmem],
        out_specs=(vmem, vmem),
        scratch_shapes=[
            pltpu.VMEM((others, 2 * rows, site_local), f32),
            pltpu.VMEM((chips, rows, site_local), f32),
            pltpu.VMEM((others, mode_total, site_local), f32),
            pltpu.VMEM((chips, mode_total, site_local), f32),
            pltpu.VMEM((verts, rows, depth), bf16),
            pltpu.VMEM((verts, rows, depth), bf16),
            pltpu.VMEM((width, depth), bf16),
            pltpu.VMEM((width, depth), bf16),
            pltpu.VMEM((verts, rows, mode_total), bf16),
            pltpu.VMEM((verts, rows, mode_total), bf16),
            pltpu.VMEM((CHUNKS, slices + 1, 2, rows, width), f32),
            pltpu.VMEM((CHUNKS, others, rows, width), f32),
            pltpu.VMEM((CHUNKS, chips, rows, width), f32),
            pltpu.VMEM((mode_total, width), bf16),
            pltpu.VMEM((mode_total, width), bf16),
            dma(others), dma(chips), dma(others, CHUNKS), dma(chips, CHUNKS),
            dma(CHUNKS, slices), dma(others, CHUNKS), dma(chips, CHUNKS),
        ],
        compiler_params=pltpu.CompilerParams(
            collective_id=0, has_side_effects=True, vmem_limit_bytes=58 * 2**20
        ),
    )(partners, phases, left_local, right_local)
    return (meson.transpose(1, 0, 2)[None], product.transpose(1, 0, 2)[None])


def solution(mesh):
    in_specs = (P(("grp", "cuts"), None, "space"), P(("grp", "cuts"), None, "space"), P(), P())
    out_specs = (P(("grp", "cuts"), "space", None, None), P(("grp", "cuts"), "space", None, None))
    return jax.shard_map(
        on_device, mesh=mesh, in_specs=in_specs, out_specs=out_specs, check_vma=False
    )
```

```python
import functools
import math

import jax
import jax.numpy as jnp
from jax import lax
from jax.experimental import pallas as pl
from jax.experimental.pallas import tpu as pltpu
from jax.sharding import PartitionSpec as P

MODES = 1024
CHUNKS = 8
PAIR = 2


def phase_table(momenta, site_total):
    global_site = jnp.arange(site_total, dtype=jnp.int32)
    coord_x = global_site % 8
    coord_y = global_site // 8 % 8
    coord_z = global_site // 64
    depth = site_total // 64
    numerator = (
        (momenta[:, 0:1] * coord_x[None] + momenta[:, 1:2] * coord_y[None]) * depth
        + momenta[:, 2:3] * coord_z[None] * 8
    ) % (8 * depth)
    return jnp.cos(2.0 * math.pi * numerator.astype(jnp.float32) / (8 * depth))


def split(value):
    high = value.astype(jnp.bfloat16)
    return high, (value - high.astype(jnp.float32)).astype(jnp.bfloat16)


def dot3(a_high, a_low, b_high, b_low, b_axis):
    dims = (((1,), (b_axis,)), ((), ()))
    dot = functools.partial(
        lax.dot_general, dimension_numbers=dims, preferred_element_type=jnp.float32
    )
    return dot(a_low, b_high) + dot(a_high, b_low) + dot(a_high, b_high)


def kernel(
    slices, space_size, scale,
    partners_ref, phase_ref, left_ref, right_ref,
    meson_ref, product_ref,
    m_held, p_held,
    left_far, left_peer, right_far, right_peer,
    w_high, w_low, r_high, r_low, m_high, m_low,
    route, field_far, field_peer, f_high, f_low,
    lf_sem, lp_sem, rf_sem, rp_sem, z_sem, ff_sem, fp_sem, m_sem, p_sem,
):
    mode_total, site_local = left_ref.shape
    verts = phase_ref.shape[0]
    rows = mode_total // space_size
    chips = space_size // 2
    width = mode_total // CHUNKS
    far = range(1, chips)

    me = lax.axis_index("space")
    zed = lax.axis_index("cuts")
    chip, core = me // 2, me % 2
    peer = chip * 2 + 1 - core

    def far_device(d):
        return lax.rem(chip + d, chips) * 2 + core

    def source(d, k):
        from_chip = lax.rem(chip + chips - d, chips)
        return from_chip * 2 + (core if k == 0 else 1 - core)

    def remote(src, dst, sems, where, axis, target):
        return pltpu.make_async_remote_copy(
            src_ref=src,
            dst_ref=dst,
            send_sem=sems.at[(0,) + where],
            recv_sem=sems.at[(1,) + where],
            device_id={axis: target},
            device_id_type=pl.DeviceIdType.MESH,
        )

    barrier = pltpu.get_barrier_semaphore()

    def greet(axis, target):
        pl.semaphore_signal(
            barrier, inc=1, device_id={axis: target}, device_id_type=pl.DeviceIdType.MESH
        )

    greet("space", peer)
    for d in far:
        greet("space", far_device(d))

    @pl.when(zed > 0)
    def _():
        greet("cuts", zed - 1)

    @pl.when(zed < slices - 1)
    def _():
        greet("cuts", zed + 1)

    ends = jnp.where(zed > 0, 1, 0) + jnp.where(zed < slices - 1, 1, 0)
    pl.semaphore_wait(barrier, chips + ends)

    def rows_of(ref, index, count):
        return ref.at[pl.ds(pl.multiple_of(index * count, count), count), :]

    def chunk_of(ref, j):
        return ref.at[pl.ds(j * width, width), :]

    left_far_copy = {
        d: remote(
            rows_of(left_ref, lax.rem(chip + d, chips), 2 * rows),
            left_far.at[d - 1], lf_sem, (d - 1,), "space", far_device(d),
        )
        for d in far
    }
    right_far_copy = {
        (d, j): remote(
            chunk_of(right_ref, j), chunk_of(right_far.at[d - 1], j),
            rf_sem, (d - 1, j), "space", far_device(d),
        )
        for d in far for j in range(CHUNKS)
    }
    left_peer_copy = {
        d: remote(
            rows_of(left_ref, peer, rows) if d == 0 else rows_of(left_far.at[d - 1], 1 - core, rows),
            left_peer.at[d], lp_sem, (d,), "space", peer,
        )
        for d in range(chips)
    }
    right_peer_copy = {
        (d, j): remote(
            chunk_of(right_ref if d == 0 else right_far.at[d - 1], j),
            chunk_of(right_peer.at[d], j), rp_sem, (d, j), "space", peer,
        )
        for d in range(chips) for j in range(CHUNKS)
    }

    def z_copy(j, r):
        up = zed % 2 == r % 2
        other = jnp.where(up, zed + 1, zed - 1)
        has = (other >= 0) & (other < slices)
        return has, remote(route.at[j, r, 0], route.at[j, r, 1], z_sem, (j, r), "cuts", other)

    field_far_copy = {
        (d, j): remote(
            route.at[j, slices, 0], field_far.at[j, d - 1], ff_sem, (d - 1, j), "space", far_device(d)
        )
        for d in far for j in range(CHUNKS)
    }
    field_peer_copy = {
        (d, j): remote(
            route.at[j, slices, 0] if d == 0 else field_far.at[j, d - 1],
            field_peer.at[j, d], fp_sem, (d, j), "space", peer,
        )
        for d in range(chips) for j in range(CHUNKS)
    }

    for d in far:
        left_far_copy[d].start()
    left_peer_copy[0].start()
    for j in range(CHUNKS):
        right_peer_copy[0, j].start()

    def send_right(*chunks):
        for j in chunks:
            for d in far:
                if j < CHUNKS:
                    right_far_copy[d, j].start()

    send_right(0)

    keys = []
    for u in range(slices):
        key = jnp.int32(0)
        for t in range(slices):
            key = key + jnp.where(partners_ref[t] == u, t, 0)
        keys.append(key)
    takes = []
    for r in range(slices):
        take = jnp.int32(0)
        for i in range(r % 2, slices - 1, 2):
            low, high = jnp.minimum(keys[i], keys[i + 1]), jnp.maximum(keys[i], keys[i + 1])
            swap = jnp.where(keys[i] > keys[i + 1], 1, 0)
            mine = jnp.where((zed == i) | (zed == i + 1), 1, 0)
            take = take + swap * mine
            keys[i], keys[i + 1] = low, high
        takes.append(take)

    def weigh(d, k, block):
        at = (2 * d + k) * site_local
        first = pl.multiple_of(source(d, k) * site_local, site_local)
        for a in range(verts):
            high, low = split(block * phase_ref[pl.ds(a, 1), pl.ds(first, site_local)])
            w_high[a, :, pl.ds(at, site_local)] = high
            w_low[a, :, pl.ds(at, site_local)] = low

    def own_rows(ref, index):
        return ref[pl.ds(pl.multiple_of(index * rows, rows), rows), :]

    weigh(0, 0, own_rows(left_ref, me))
    left_peer_copy[0].wait_recv()
    weigh(0, 1, left_peer[0])
    for d in far:
        left_far_copy[d].wait_recv()
        left_peer_copy[d].start()
        if d == chips - 1:
            send_right(1, 2)
        weigh(d, 0, own_rows(left_far.at[d - 1], core))
    for d in far:
        left_peer_copy[d].wait_recv()
        weigh(d, 1, left_peer[d])

    def split_right(d, k, j, block):
        at = (2 * d + k) * site_local
        high, low = split(block)
        r_high[pl.ds(j % PAIR * width, width), pl.ds(at, site_local)] = high
        r_low[pl.ds(j % PAIR * width, width), pl.ds(at, site_local)] = low

    def meson_block(a, j, count):
        some = pl.ds(j % PAIR * width, count * width)
        block = dot3(w_high[a], w_low[a], r_high[some, :], r_low[some, :], 1)
        columns = pl.ds(j * width, count * width)
        m_held[a, :, columns] = block
        high, low = split(block)
        m_high[a, :, columns] = high
        m_low[a, :, columns] = low
        return block

    def z_start(j, r):
        has, copy = z_copy(j, r)

        @pl.when(has)
        def _():
            copy.start()

    def fields(j):
        split_right(0, 0, j, right_ref[pl.ds(j * width, width), :])
        right_peer_copy[0, j].wait_recv()
        split_right(0, 1, j, right_peer[0, pl.ds(j * width, width), :])
        for d in far:
            right_far_copy[d, j].wait_recv()
            right_peer_copy[d, j].start()
            if d == chips - 1 and j > 0:
                send_right(j + 2)
            split_right(d, 0, j, right_far[d - 1, pl.ds(j * width, width), :])
        for d in far:
            right_peer_copy[d, j].wait_recv()
            split_right(d, 1, j, right_peer[d, pl.ds(j * width, width), :])
        route[j, 0, 0] = meson_block(0, j, 1)
        z_start(j, 0)

    def out_copy(held, ref, sems, a, g):
        columns = pl.ds(g * PAIR * width, PAIR * width)
        return pltpu.make_async_copy(
            held.at[a, :, columns], ref.at[:, a, columns], sems.at[a, g]
        )

    def other_fields(g):
        def other_vertex(a, carry):
            meson_block(a, g * PAIR, PAIR)
            return carry

        lax.fori_loop(1, verts, other_vertex, 0)
        for a in range(verts):
            out_copy(m_held, meson_ref, m_sem, a, g).start()

    def z_round(j, r):
        has, copy = z_copy(j, r)

        @pl.when(has)
        def _():
            copy.wait_recv()
            taken = jnp.full((rows, width), takes[r], jnp.int32) > 0
            route[j, r + 1, 0] = jnp.where(taken, route[j, r, 1], route[j, r, 0])

        @pl.when(jnp.logical_not(has))
        def _():
            route[j, r + 1, 0] = route[j, r, 0]

        if r + 1 < slices:
            z_start(j, r + 1)
        else:
            for d in far:
                field_far_copy[d, j].start()
            field_peer_copy[0, j].start()

    def pass_on(j):
        for d in far:
            field_far_copy[d, j].wait_recv()
            field_peer_copy[d, j].start()

    def gathered(j):
        def place(d, k, block):
            first = pl.multiple_of(source(d, k) * rows, rows)
            high, low = split(block)
            f_high[pl.ds(first, rows), pl.ds(j % PAIR * width, width)] = high
            f_low[pl.ds(first, rows), pl.ds(j % PAIR * width, width)] = low

        place(0, 0, route[j, slices, 0])
        for d in far:
            place(d, 0, field_far[j, d - 1])
        for d in range(chips):
            field_peer_copy[d, j].wait_recv()
            place(d, 1, field_peer[j, d])

    def products(g):
        def vertex(a, carry):
            block = dot3(m_high[a], m_low[a], f_high[...], f_low[...], 0)
            p_held[a, :, pl.ds(g * PAIR * width, PAIR * width)] = block * scale
            return carry

        lax.fori_loop(0, verts, vertex, 0)
        for a in range(verts):
            out_copy(p_held, product_ref, p_sem, a, g).start()

    for step in range(CHUNKS + slices + 2):
        if step < CHUNKS:
            fields(step)
        for r in reversed(range(slices)):
            if 0 <= step - 1 - r < CHUNKS:
                z_round(step - 1 - r, r)
        if 0 <= step - 1 - slices < CHUNKS:
            pass_on(step - 1 - slices)
        if step < CHUNKS and step % PAIR == PAIR - 1:
            other_fields(step // PAIR)
        j = step - 2 - slices
        if 0 <= j < CHUNKS:
            gathered(j)
            if j % PAIR == PAIR - 1:
                products(j // PAIR)

    for g in range(CHUNKS // PAIR):
        for a in range(verts):
            out_copy(m_held, meson_ref, m_sem, a, g).wait()
            out_copy(p_held, product_ref, p_sem, a, g).wait()
    for copies in (
        left_far_copy, right_far_copy, left_peer_copy, right_peer_copy,
        field_far_copy, field_peer_copy,
    ):
        for copy in copies.values():
            copy.wait_send()
    for j in range(CHUNKS):
        for r in range(slices):
            has, copy = z_copy(j, r)

            @pl.when(has)
            def _(copy=copy):
                copy.wait_send()


def on_device(left_modes, right_modes, momenta, partners):
    left_local, right_local = left_modes[0], right_modes[0]
    mode_total, site_local = left_local.shape
    space_size = lax.axis_size("space")
    slices = lax.axis_size("cuts")
    verts = momenta.shape[0]
    rows = mode_total // space_size
    chips = space_size // 2
    others = max(chips - 1, 1)
    width = mode_total // CHUNKS
    depth = site_local * space_size
    phases = phase_table(momenta, depth)
    f32, bf16 = jnp.float32, jnp.bfloat16
    vmem = pl.BlockSpec(memory_space=pltpu.VMEM)
    out = jax.ShapeDtypeStruct((rows, verts, mode_total), f32)
    hbm = pl.BlockSpec(memory_space=pl.ANY)

    def dma(*shape):
        return pltpu.SemaphoreType.DMA((2,) + shape)

    meson, product = pl.pallas_call(
        functools.partial(kernel, slices, space_size, 1.0 / math.sqrt(mode_total)),
        out_shape=(out, out),
        in_specs=[pl.BlockSpec(memory_space=pltpu.SMEM), vmem, vmem, vmem],
        out_specs=(hbm, hbm),
        scratch_shapes=[
            pltpu.VMEM((verts, rows, mode_total), f32),
            pltpu.VMEM((verts, rows, mode_total), f32),
            pltpu.VMEM((others, 2 * rows, site_local), f32),
            pltpu.VMEM((chips, rows, site_local), f32),
            pltpu.VMEM((others, mode_total, site_local), f32),
            pltpu.VMEM((chips, mode_total, site_local), f32),
            pltpu.VMEM((verts, rows, depth), bf16),
            pltpu.VMEM((verts, rows, depth), bf16),
            pltpu.VMEM((PAIR * width, depth), bf16),
            pltpu.VMEM((PAIR * width, depth), bf16),
            pltpu.VMEM((verts, rows, mode_total), bf16),
            pltpu.VMEM((verts, rows, mode_total), bf16),
            pltpu.VMEM((CHUNKS, slices + 1, 2, rows, width), f32),
            pltpu.VMEM((CHUNKS, others, rows, width), f32),
            pltpu.VMEM((CHUNKS, chips, rows, width), f32),
            pltpu.VMEM((mode_total, PAIR * width), bf16),
            pltpu.VMEM((mode_total, PAIR * width), bf16),
            dma(others), dma(chips), dma(others, CHUNKS), dma(chips, CHUNKS),
            dma(CHUNKS, slices), dma(others, CHUNKS), dma(chips, CHUNKS),
            pltpu.SemaphoreType.DMA((verts, CHUNKS // PAIR)),
            pltpu.SemaphoreType.DMA((verts, CHUNKS // PAIR)),
        ],
        compiler_params=pltpu.CompilerParams(
            collective_id=0, has_side_effects=True, vmem_limit_bytes=58 * 2**20
        ),
    )(partners, phases, left_local, right_local)
    return (meson[None], product[None])


def solution(mesh):
    in_specs = (P(("grp", "cuts"), None, "space"), P(("grp", "cuts"), None, "space"), P(), P())
    out_specs = (P(("grp", "cuts"), "space", None, None), P(("grp", "cuts"), "space", None, None))
    return jax.shard_map(
        on_device, mesh=mesh, in_specs=in_specs, out_specs=out_specs, check_vma=False
    )
```

```python
import functools
import math

import jax
import jax.numpy as jnp
from jax import lax
from jax.experimental import pallas as pl
from jax.experimental.pallas import tpu as pltpu
from jax.sharding import PartitionSpec as P

MODES = 1024
CHUNKS = 8
PAIR = 2


def phase_table(momenta, site_total):
    global_site = jnp.arange(site_total, dtype=jnp.int32)
    coord_x = global_site % 8
    coord_y = global_site // 8 % 8
    coord_z = global_site // 64
    depth = site_total // 64
    numerator = (
        (momenta[:, 0:1] * coord_x[None] + momenta[:, 1:2] * coord_y[None]) * depth
        + momenta[:, 2:3] * coord_z[None] * 8
    ) % (8 * depth)
    return jnp.cos(2.0 * math.pi * numerator.astype(jnp.float32) / (8 * depth))


def split(value):
    high = value.astype(jnp.bfloat16)
    return high, (value - high.astype(jnp.float32)).astype(jnp.bfloat16)


def dot3(a_high, a_low, b_high, b_low, b_axis):
    dims = (((1,), (b_axis,)), ((), ()))
    dot = functools.partial(
        lax.dot_general, dimension_numbers=dims, preferred_element_type=jnp.float32
    )
    return dot(a_low, b_high) + dot(a_high, b_low) + dot(a_high, b_high)


def kernel(
    slices, space_size, scale,
    partners_ref, phase_ref, left_ref, right_ref,
    meson_ref, product_ref,
    m_held, p_held,
    left_far, left_peer, right_far, right_peer,
    w_high, w_low, r_high, r_low, m_high, m_low,
    route, field_far, field_peer, f_high, f_low,
    lf_sem, lp_sem, rf_sem, rp_sem, z_sem, ff_sem, fp_sem, m_sem, p_sem,
):
    mode_total, site_local = left_ref.shape
    verts = phase_ref.shape[0]
    rows = mode_total // space_size
    chips = space_size // 2
    width = mode_total // CHUNKS
    far = range(1, chips)

    me = lax.axis_index("space")
    zed = lax.axis_index("cuts")
    chip, core = me // 2, me % 2
    peer = chip * 2 + 1 - core

    def far_device(d):
        return lax.rem(chip + d, chips) * 2 + core

    def source(d, k):
        from_chip = lax.rem(chip + chips - d, chips)
        return from_chip * 2 + (core if k == 0 else 1 - core)

    def remote(src, dst, sems, where, axis, target):
        return pltpu.make_async_remote_copy(
            src_ref=src,
            dst_ref=dst,
            send_sem=sems.at[(0,) + where],
            recv_sem=sems.at[(1,) + where],
            device_id={axis: target},
            device_id_type=pl.DeviceIdType.MESH,
        )

    barrier = pltpu.get_barrier_semaphore()

    def greet(axis, target):
        pl.semaphore_signal(
            barrier, inc=1, device_id={axis: target}, device_id_type=pl.DeviceIdType.MESH
        )

    greet("space", peer)
    for d in far:
        greet("space", far_device(d))

    @pl.when(zed > 0)
    def _():
        greet("cuts", zed - 1)

    @pl.when(zed < slices - 1)
    def _():
        greet("cuts", zed + 1)

    ends = jnp.where(zed > 0, 1, 0) + jnp.where(zed < slices - 1, 1, 0)
    pl.semaphore_wait(barrier, chips + ends)

    def rows_of(ref, index, count):
        return ref.at[pl.ds(pl.multiple_of(index * count, count), count), :]

    def chunk_of(ref, j):
        return ref.at[pl.ds(j * width, width), :]

    left_far_copy = {
        d: remote(
            rows_of(left_ref, lax.rem(chip + d, chips), 2 * rows),
            left_far.at[d - 1], lf_sem, (d - 1,), "space", far_device(d),
        )
        for d in far
    }
    right_far_copy = {
        (d, j): remote(
            chunk_of(right_ref, j), chunk_of(right_far.at[d - 1], j),
            rf_sem, (d - 1, j), "space", far_device(d),
        )
        for d in far for j in range(CHUNKS)
    }
    left_peer_copy = {
        d: remote(
            rows_of(left_ref, peer, rows) if d == 0 else rows_of(left_far.at[d - 1], 1 - core, rows),
            left_peer.at[d], lp_sem, (d,), "space", peer,
        )
        for d in range(chips)
    }
    right_peer_copy = {
        (d, j): remote(
            chunk_of(right_ref if d == 0 else right_far.at[d - 1], j),
            chunk_of(right_peer.at[d], j), rp_sem, (d, j), "space", peer,
        )
        for d in range(chips) for j in range(CHUNKS)
    }

    def z_copy(j, r):
        up = zed % 2 == r % 2
        other = jnp.where(up, zed + 1, zed - 1)
        has = (other >= 0) & (other < slices)
        return has, remote(route.at[j, r, 0], route.at[j, r, 1], z_sem, (j, r), "cuts", other)

    field_far_copy = {
        (d, j): remote(
            route.at[j, slices, 0], field_far.at[j, d - 1], ff_sem, (d - 1, j), "space", far_device(d)
        )
        for d in far for j in range(CHUNKS)
    }
    field_peer_copy = {
        (d, j): remote(
            route.at[j, slices, 0] if d == 0 else field_far.at[j, d - 1],
            field_peer.at[j, d], fp_sem, (d, j), "space", peer,
        )
        for d in range(chips) for j in range(CHUNKS)
    }

    for d in far:
        left_far_copy[d].start()
    left_peer_copy[0].start()
    for j in range(CHUNKS):
        right_peer_copy[0, j].start()

    def send_right(*chunks):
        for j in chunks:
            for d in far:
                if j < CHUNKS:
                    right_far_copy[d, j].start()

    send_right(0)

    keys = []
    for u in range(slices):
        key = jnp.int32(0)
        for t in range(slices):
            key = key + jnp.where(partners_ref[t] == u, t, 0)
        keys.append(key)
    takes = []
    for r in range(slices):
        take = jnp.int32(0)
        for i in range(r % 2, slices - 1, 2):
            low, high = jnp.minimum(keys[i], keys[i + 1]), jnp.maximum(keys[i], keys[i + 1])
            swap = jnp.where(keys[i] > keys[i + 1], 1, 0)
            mine = jnp.where((zed == i) | (zed == i + 1), 1, 0)
            take = take + swap * mine
            keys[i], keys[i + 1] = low, high
        takes.append(take)

    def weigh(d, k, block):
        at = (2 * d + k) * site_local
        first = pl.multiple_of(source(d, k) * site_local, site_local)
        for a in range(verts):
            high, low = split(block * phase_ref[pl.ds(a, 1), pl.ds(first, site_local)])
            w_high[a, :, pl.ds(at, site_local)] = high
            w_low[a, :, pl.ds(at, site_local)] = low

    def own_rows(ref, index):
        return ref[pl.ds(pl.multiple_of(index * rows, rows), rows), :]

    weigh(0, 0, own_rows(left_ref, me))
    left_peer_copy[0].wait_recv()
    weigh(0, 1, left_peer[0])
    for d in far:
        left_far_copy[d].wait_recv()
        left_peer_copy[d].start()
        if d == chips - 1:
            send_right(1, 2)
        weigh(d, 0, own_rows(left_far.at[d - 1], core))
    for d in far:
        left_peer_copy[d].wait_recv()
        weigh(d, 1, left_peer[d])

    def split_right(d, k, j, block):
        at = (2 * d + k) * site_local
        high, low = split(block)
        r_high[pl.ds(j % PAIR * width, width), pl.ds(at, site_local)] = high
        r_low[pl.ds(j % PAIR * width, width), pl.ds(at, site_local)] = low

    def meson_block(a, j, count):
        some = pl.ds(j % PAIR * width, count * width)
        block = dot3(w_high[a], w_low[a], r_high[some, :], r_low[some, :], 1)
        columns = pl.ds(j * width, count * width)
        m_held[a, :, columns] = block
        high, low = split(block)
        m_high[a, :, columns] = high
        m_low[a, :, columns] = low
        return block

    def z_start(j, r):
        has, copy = z_copy(j, r)

        @pl.when(has)
        def _():
            copy.start()

    def fields(j):
        split_right(0, 0, j, right_ref[pl.ds(j * width, width), :])
        right_peer_copy[0, j].wait_recv()
        split_right(0, 1, j, right_peer[0, pl.ds(j * width, width), :])
        for d in far:
            right_far_copy[d, j].wait_recv()
            right_peer_copy[d, j].start()
            if d == chips - 1 and j > 0:
                send_right(j + 2)
            split_right(d, 0, j, right_far[d - 1, pl.ds(j * width, width), :])
        for d in far:
            right_peer_copy[d, j].wait_recv()
            split_right(d, 1, j, right_peer[d, pl.ds(j * width, width), :])
        route[j, 0, 0] = meson_block(0, j, 1)
        z_start(j, 0)

    def out_copy(held, ref, sems, a, g):
        columns = pl.ds(g * PAIR * width, PAIR * width)
        return pltpu.make_async_copy(
            held.at[a, :, columns], ref.at[:, a, columns], sems.at[a, g]
        )

    def other_fields(g):
        def other_vertex(a, carry):
            meson_block(a, g * PAIR, PAIR)
            return carry

        lax.fori_loop(1, verts, other_vertex, 0)
        for a in range(verts):
            out_copy(m_held, meson_ref, m_sem, a, g).start()

    def z_round(j, r):
        has, copy = z_copy(j, r)

        @pl.when(has)
        def _():
            copy.wait_recv()
            taken = jnp.full((rows, width), takes[r], jnp.int32) > 0
            route[j, r + 1, 0] = jnp.where(taken, route[j, r, 1], route[j, r, 0])

        @pl.when(jnp.logical_not(has))
        def _():
            route[j, r + 1, 0] = route[j, r, 0]

        if r + 1 < slices:
            z_start(j, r + 1)
        else:
            for d in far:
                field_far_copy[d, j].start()
            field_peer_copy[0, j].start()

    def pass_on(j):
        for d in far:
            field_far_copy[d, j].wait_recv()
            field_peer_copy[d, j].start()

    def gathered(j):
        def place(d, k, block):
            first = pl.multiple_of(source(d, k) * rows, rows)
            high, low = split(block)
            f_high[pl.ds(first, rows), pl.ds(j % PAIR * width, width)] = high
            f_low[pl.ds(first, rows), pl.ds(j % PAIR * width, width)] = low

        place(0, 0, route[j, slices, 0])
        for d in far:
            place(d, 0, field_far[j, d - 1])
        for d in range(chips):
            field_peer_copy[d, j].wait_recv()
            place(d, 1, field_peer[j, d])

    def products(g):
        def vertex(a, carry):
            block = dot3(m_high[a], m_low[a], f_high[...], f_low[...], 0)
            p_held[a, :, pl.ds(g * PAIR * width, PAIR * width)] = block * scale
            return carry

        lax.fori_loop(0, verts, vertex, 0)
        for a in range(verts):
            out_copy(p_held, product_ref, p_sem, a, g).start()

    for step in range(CHUNKS + 2 * slices + 2):
        if step < CHUNKS:
            fields(step)
        for r in reversed(range(slices)):
            if 0 <= step - 1 - 2 * r < CHUNKS:
                z_round(step - 1 - 2 * r, r)
        if 0 <= step - 2 - 2 * (slices - 1) < CHUNKS:
            pass_on(step - 2 - 2 * (slices - 1))
        if step < CHUNKS and step % PAIR == PAIR - 1:
            other_fields(step // PAIR)
        j = step - 3 - 2 * (slices - 1)
        if 0 <= j < CHUNKS:
            gathered(j)
            if j % PAIR == PAIR - 1:
                products(j // PAIR)

    for g in range(CHUNKS // PAIR):
        for a in range(verts):
            out_copy(m_held, meson_ref, m_sem, a, g).wait()
            out_copy(p_held, product_ref, p_sem, a, g).wait()
    for copies in (
        left_far_copy, right_far_copy, left_peer_copy, right_peer_copy,
        field_far_copy, field_peer_copy,
    ):
        for copy in copies.values():
            copy.wait_send()
    for j in range(CHUNKS):
        for r in range(slices):
            has, copy = z_copy(j, r)

            @pl.when(has)
            def _(copy=copy):
                copy.wait_send()


def on_device(left_modes, right_modes, momenta, partners):
    left_local, right_local = left_modes[0], right_modes[0]
    mode_total, site_local = left_local.shape
    space_size = lax.axis_size("space")
    slices = lax.axis_size("cuts")
    verts = momenta.shape[0]
    rows = mode_total // space_size
    chips = space_size // 2
    others = max(chips - 1, 1)
    width = mode_total // CHUNKS
    depth = site_local * space_size
    phases = phase_table(momenta, depth)
    f32, bf16 = jnp.float32, jnp.bfloat16
    vmem = pl.BlockSpec(memory_space=pltpu.VMEM)
    out = jax.ShapeDtypeStruct((rows, verts, mode_total), f32)
    hbm = pl.BlockSpec(memory_space=pl.ANY)

    def dma(*shape):
        return pltpu.SemaphoreType.DMA((2,) + shape)

    meson, product = pl.pallas_call(
        functools.partial(kernel, slices, space_size, 1.0 / math.sqrt(mode_total)),
        out_shape=(out, out),
        in_specs=[pl.BlockSpec(memory_space=pltpu.SMEM), vmem, vmem, vmem],
        out_specs=(hbm, hbm),
        scratch_shapes=[
            pltpu.VMEM((verts, rows, mode_total), f32),
            pltpu.VMEM((verts, rows, mode_total), f32),
            pltpu.VMEM((others, 2 * rows, site_local), f32),
            pltpu.VMEM((chips, rows, site_local), f32),
            pltpu.VMEM((others, mode_total, site_local), f32),
            pltpu.VMEM((chips, mode_total, site_local), f32),
            pltpu.VMEM((verts, rows, depth), bf16),
            pltpu.VMEM((verts, rows, depth), bf16),
            pltpu.VMEM((PAIR * width, depth), bf16),
            pltpu.VMEM((PAIR * width, depth), bf16),
            pltpu.VMEM((verts, rows, mode_total), bf16),
            pltpu.VMEM((verts, rows, mode_total), bf16),
            pltpu.VMEM((CHUNKS, slices + 1, 2, rows, width), f32),
            pltpu.VMEM((CHUNKS, others, rows, width), f32),
            pltpu.VMEM((CHUNKS, chips, rows, width), f32),
            pltpu.VMEM((mode_total, PAIR * width), bf16),
            pltpu.VMEM((mode_total, PAIR * width), bf16),
            dma(others), dma(chips), dma(others, CHUNKS), dma(chips, CHUNKS),
            dma(CHUNKS, slices), dma(others, CHUNKS), dma(chips, CHUNKS),
            pltpu.SemaphoreType.DMA((verts, CHUNKS // PAIR)),
            pltpu.SemaphoreType.DMA((verts, CHUNKS // PAIR)),
        ],
        compiler_params=pltpu.CompilerParams(
            collective_id=0, has_side_effects=True, vmem_limit_bytes=58 * 2**20
        ),
    )(partners, phases, left_local, right_local)
    return (meson[None], product[None])


def solution(mesh):
    in_specs = (P(("grp", "cuts"), None, "space"), P(("grp", "cuts"), None, "space"), P(), P())
    out_specs = (P(("grp", "cuts"), "space", None, None), P(("grp", "cuts"), "space", None, None))
    return jax.shard_map(
        on_device, mesh=mesh, in_specs=in_specs, out_specs=out_specs, check_vma=False
    )
```
